512 devices in a mesh: grp: 8 (over z_hi, core), seq: 8 (over z_lo, x), tp: 8 (over y).
Axes of the slice: x: 4, y: 8, z: 8 (z_hi: 4, z_lo: 2; z = z_hi * 2 + z_lo), core: 2. Of those that a mesh axis runs over, the one named last changes fastest.
Arguments:
- queries: bfloat16 [4, 2048, 8192], P(None, ('grp', 'seq'), 'tp'), may hold values from -6 to 6
- new_token_cache: bfloat16 [4, 2048, 2048], P(None, ('grp', 'seq'), 'tp'), may hold values from -6 to 6
- kv_pool: bfloat16 [4096, 16, 2048], P(('grp', 'seq'), None, 'tp'), may hold values from -6 to 6
- block_table: int32 [2048, 2], P(('grp', 'seq')), may hold values from 0 to 63, as said below
- context_len: int32 [64, 32], P(('grp', 'seq')), may hold values from 1 to 32, 512 in all within a row
- out_proj: bfloat16 [8192, 8192], P('tp', 'seq'), may hold values from -0.09375 to 0.09375
- finished_prompt_cache: bfloat16 [4096, 16, 2048], P(('grp', 'seq'), None, 'tp'), may hold values from -6 to 6
- prompt_blocks: int32 [64, 32], P(('grp', 'seq')), may hold values from 1 to 3, as said below
- prompt_tail: int32 [64, 32], P(('grp', 'seq')), may hold values from 1 to 16
- prompt_owner: int32 [64, 32], P(('grp', 'seq')), may hold values from 0 to 63, as said below
Outputs:
- decoded: bfloat16 [4, 2048, 8192], P(None, 'grp', ('seq', 'tp'))
- migrated: bfloat16 [12288, 16, 2048], P(('grp', 'seq'), None, 'tp')
The draws below stay inside these ranges and needn't reach their ends.
Inputs may be any that keep to these rules, and one draw needn't show every extreme that they name: `block_table`: within the 32 rows of each device the entries are a permutation of the device's local page numbers 0 to 63. `context_len`: the 32 lengths of one device sum to half of 1024. `prompt_blocks`: the 32 entries of one device sum to 64; the first prompt of every device has 3 blocks. `prompt_owner`: the 32 owners of one device are distinct; the first prompts of all devices have one common owner.
All inputs are finite; a program needn't handle non-finite values.
Results may differ from the reference program's by a relative error of at most 0.015.
Values may be sent and summed in bfloat16 or wider, within the bound.
No kernel may reach another device: no remote copies, remote signals or barrier semaphores. Data moves between devices by JAX's collectives and lax.ppermute only.
A program may use at most 64 MiB of HBM per device.

```python
import math
import jax
import jax.numpy as jnp
import numpy as np
from jax import lax

D = 8192
QUERY_HEADS = 64
KEY_VALUE_HEADS = 8
HEAD_SIZE = 128
DECODE_STEPS = 4
PAGE_TOKENS = 16
CAP = 3
RQ_DEV = 32
MAXP = 2
PEER_DEVICES = 64
DECODE_REQUESTS = 2048
DEVICE_PAGES = 64
PR_DEV = 32
P_DEV = 64
PROMPT_BLOCKS = 4096
RECEIVE_SLOTS = 12288


def draw_queries(key, part):
    key = jax.random.fold_in(key, 2)
    base_offset = jnp.clip(jax.random.normal(jax.random.fold_in(key, 1), (DECODE_STEPS, DECODE_REQUESTS, QUERY_HEADS * HEAD_SIZE), jnp.float32), -6.0, 6.0)
    return base_offset.astype(jnp.bfloat16)


def draw_kv_pool(key, part):
    key = jax.random.fold_in(key, 1)
    array_shape = (PEER_DEVICES * DEVICE_PAGES, PAGE_TOKENS, KEY_VALUE_HEADS, 2, HEAD_SIZE)
    base_offset = jnp.clip(jax.random.normal(jax.random.fold_in(key, 5), array_shape, jnp.float32), -6.0, 6.0)
    return base_offset.reshape(PEER_DEVICES * DEVICE_PAGES, PAGE_TOKENS, KEY_VALUE_HEADS * 2 * HEAD_SIZE).astype(jnp.bfloat16)


def draw_block_table(key, part):
    key = jax.random.fold_in(key, 3)

    def one_device(device):
        return jax.random.permutation(jax.random.fold_in(key, device), DEVICE_PAGES).astype(jnp.int32).reshape(RQ_DEV, MAXP)
    tables = jax.vmap(one_device)(jnp.arange(PEER_DEVICES, dtype=jnp.int32))
    return tables.reshape(DECODE_REQUESTS, MAXP)


def draw_prompt_blocks(key, part):
    key = jax.random.fold_in(key, 11)
    others = PR_DEV - 1

    def one_device(device):
        inner = jax.random.fold_in(key, device)
        longer = jax.random.randint(jax.random.fold_in(inner, 1), (), 0, (PR_DEV - 2) // 2 + 1)
        order = jnp.arange(others, dtype=jnp.int32)
        runs = jnp.where(order < longer, CAP, jnp.where(order < 2 * longer + 1, CAP - 2, CAP - 1)).astype(jnp.int32)
        runs = jax.random.permutation(jax.random.fold_in(inner, 2), runs)
        return jnp.concatenate([jnp.full((1,), CAP, jnp.int32), runs]).astype(jnp.int32)
    return jax.vmap(one_device)(jnp.arange(PEER_DEVICES, dtype=jnp.int32))


def draw_prompt_owner(key, part):
    key = jax.random.fold_in(key, 12)
    common = jax.random.randint(jax.random.fold_in(key, 1), (), 0, PEER_DEVICES).astype(jnp.int32)

    def one_device(device):
        order = jax.random.permutation(jax.random.fold_in(key, device + 2), PEER_DEVICES - 1).astype(jnp.int32)
        others = order[:PR_DEV - 1]
        others = (others + (others >= common).astype(jnp.int32)).astype(jnp.int32)
        return jnp.concatenate([common[None], others]).astype(jnp.int32)
    return jax.vmap(one_device)(jnp.arange(PEER_DEVICES, dtype=jnp.int32))


def touch_ends(drawn, own_key, low, largest):
    extent = drawn.shape
    index_at = [jax.random.randint(jax.random.fold_in(own_key, axis), (), 0, extent[axis]) for axis in range(len(extent))]
    drawn = drawn.at[tuple(index_at)].set(low)
    longest = extent.index(max(extent))
    index_at[longest] = (index_at[longest] + 1) % extent[longest]
    return drawn.at[tuple(index_at)].set(largest)


def strengthened(entries, own_key, source, target, shards_of, factor):
    owner, partner = [(jnp.arange(entries.shape[position]) // (entries.shape[position] // shards_of)).reshape([-1 if axis == position else 1 for axis in range(entries.ndim)]) for position in (source, target)]
    chosen = jax.random.permutation(own_key, shards_of)[partner]
    strong = (owner == chosen) | (owner == (partner + shards_of // 2) % shards_of)
    return jnp.where(strong, factor * entries, entries)


def shard_levels(own_key, shape, cuts, smallest, top_value):
    def one(axis_at, shards_of):
        heights = jax.random.uniform(jax.random.fold_in(jax.random.fold_in(own_key, 6), axis_at), (shards_of,), jnp.float32, smallest / len(cuts), top_value / len(cuts))
        return jnp.repeat(jnp.exp(heights), shape[axis_at] // shards_of).reshape((-1,) + (1,) * (len(shape) - axis_at - 1))

    factor_of = one(*cuts[0])
    for cut in cuts[1:]:
        factor_of = factor_of * one(*cut)
    return factor_of


def split_up(count, total, bound, skew):
    portions = [(1 << 20) // math.isqrt(rank ** skew) + 1 for rank in range(2, count + 1)]
    spare, holding = total - bound - (count - 1), [1] * (count - 1)
    while spare > 0:
        movable = [i for i in range(count - 1) if holding[i] < bound]
        pool, budget = sum([portions[i] for i in movable]), spare
        for i in movable:
            addition = min(bound - holding[i], max(1, budget * portions[i] // pool), spare)
            holding[i] = holding[i] + addition
            spare = spare - addition
    return np.array([bound] + holding)


def ragged_sizes(key, number_of, total, bound, skew):
    if number_of == 2:
        one = jax.random.randint(key, (), max(1, total - bound), min(bound, total - 1) + 1)
        return jnp.stack([one, total - one])
    lengths = jnp.asarray(split_up(number_of, total, bound, skew), jnp.int32)
    twos = (number_of - 1) // 2
    giver, taker = lengths[1:1 + 2 * twos:2], lengths[2:2 + 2 * twos:2]
    margin = jnp.minimum(giver - 1, bound - taker)
    moved = jax.random.randint(jax.random.fold_in(key, 1), (twos,), 0, 1 << 20) % (margin + 1)
    lengths = lengths.at[1:1 + 2 * twos:2].set(giver - moved).at[2:2 + 2 * twos:2].set(taker + moved)
    return lengths[jax.random.permutation(jax.random.fold_in(key, 2), number_of)]


def bell_draw(own_key, dims, width, limit, shards=(), kind=jnp.bfloat16):
    array = width * jax.random.normal(own_key, dims, jnp.float32)
    if shards:
        array = array * shard_levels(own_key, dims, shards, -0.22, 0.18)
    return jnp.clip(array, -limit, limit).astype(kind)


def bell_draw_with(key, dims, deviation, limit, split, heavy, held_as=jnp.bfloat16):
    result = deviation * jax.random.normal(key, dims, jnp.float32)
    if split:
        result = result * shard_levels(key, dims, split, -0.22, 0.18)
    return jnp.clip(strengthened(result, jax.random.fold_in(key, 3), *heavy), -limit, limit).astype(held_as)


def setup_inputs(seed: int = 0) -> dict:
    key_list = jax.random.split(jax.random.key(seed), 11)
    queries = draw_queries(jax.random.fold_in(key_list[10], 71), 0)
    new_token_cache = bell_draw(key_list[1], (DECODE_STEPS, DECODE_REQUESTS, KEY_VALUE_HEADS * 2 * HEAD_SIZE), 1.0, 6.0, ((1, 64), (2, 8)))
    kv_pool = draw_kv_pool(jax.random.fold_in(key_list[10], 71), 0)
    block_table = draw_block_table(jax.random.fold_in(key_list[10], 71), 0)
    context_len = jax.vmap(lambda own: ragged_sizes(own, RQ_DEV, RQ_DEV * MAXP * PAGE_TOKENS // 2, MAXP * PAGE_TOKENS, 2))(jax.random.split(key_list[4], PEER_DEVICES)).reshape((PEER_DEVICES, RQ_DEV)).astype(jnp.int32)
    out_proj = bell_draw_with(key_list[5], (QUERY_HEADS * HEAD_SIZE, D), (QUERY_HEADS * HEAD_SIZE) ** -0.5, 0.09375, ((0, 8), (1, 8)), (0, 1, 8, 2.0))
    finished_prompt_cache = bell_draw(key_list[6], (PROMPT_BLOCKS, PAGE_TOKENS, KEY_VALUE_HEADS * 2 * HEAD_SIZE), 1.0, 6.0, ((0, 64), (2, 8)))
    prompt_blocks = draw_prompt_blocks(jax.random.fold_in(key_list[10], 71), 0)
    prompt_tail = touch_ends(jax.random.randint(key_list[8], (PEER_DEVICES, PR_DEV), 1, PAGE_TOKENS + 1), jax.random.fold_in(key_list[8], 1), 1, PAGE_TOKENS).astype(jnp.int32)
    prompt_owner = draw_prompt_owner(jax.random.fold_in(key_list[10], 71), 0)
    return dict(queries=queries, new_token_cache=new_token_cache, kv_pool=kv_pool, block_table=block_table, context_len=context_len, out_proj=out_proj, finished_prompt_cache=finished_prompt_cache, prompt_blocks=prompt_blocks, prompt_tail=prompt_tail, prompt_owner=prompt_owner)


NEGATIVE = -1e30


def attend(query_block, fresh_block, pool_block, table_block, length_row):
    steps = query_block.shape[0]
    rows = query_block.shape[1]
    kv_heads = pool_block.shape[2] // (2 * HEAD_SIZE)
    head_groups = QUERY_HEADS // KEY_VALUE_HEADS
    context = table_block.shape[1] * pool_block.shape[1]
    gathered = pool_block[table_block].reshape(rows, context, kv_heads, 2, HEAD_SIZE).astype(jnp.float32)
    key_rows = gathered[:, :, :, 0, :]
    value_rows = gathered[:, :, :, 1, :]
    fresh = fresh_block.reshape(steps, rows, kv_heads, 2, HEAD_SIZE).astype(jnp.float32)
    fresh_keys = fresh[:, :, :, 0, :]
    fresh_values = fresh[:, :, :, 1, :]
    query_heads = query_block.reshape(steps, rows, kv_heads, head_groups, HEAD_SIZE).astype(jnp.float32)
    scale = HEAD_SIZE ** -0.5
    cached = jnp.einsum("srhgd,rchd->srhgc", query_heads, key_rows) * scale
    recent = jnp.einsum("srhgd,urhd->srhgu", query_heads, fresh_keys) * scale
    live_cached = jnp.arange(context)[None, :] < length_row[:, None]
    live_cached = jnp.broadcast_to(live_cached[None, :, None, None, :], cached.shape)
    live_recent = jnp.arange(steps)[None, :] <= jnp.arange(steps)[:, None]
    live_recent = jnp.broadcast_to(live_recent[:, None, None, None, :], recent.shape)
    scores = jnp.concatenate([cached, recent], -1)
    live = jnp.concatenate([live_cached, live_recent], -1)
    masked_scores = jnp.where(live, scores, NEGATIVE)
    row_max = jnp.max(masked_scores, -1, keepdims=True)
    raw = jnp.where(live, jnp.exp(masked_scores - row_max), 0.0)
    probs = (raw / jnp.sum(raw, -1, keepdims=True)).astype(jnp.bfloat16).astype(jnp.float32)
    mixed = jnp.einsum("srhgc,rchd->srhgd", probs[..., :context], value_rows)
    mixed = mixed + jnp.einsum("srhgu,urhd->srhgd", probs[..., context:], fresh_values)
    return mixed.astype(jnp.bfloat16).reshape(steps, rows, kv_heads * head_groups * HEAD_SIZE)


def reference(queries, new_token_cache, kv_pool, block_table, context_len, out_proj, finished_prompt_cache, prompt_blocks, prompt_tail, prompt_owner):
    def per_device(device):
        query_block = lax.dynamic_slice_in_dim(queries, device * RQ_DEV, RQ_DEV, 1)
        fresh_block = lax.dynamic_slice_in_dim(new_token_cache, device * RQ_DEV, RQ_DEV, 1)
        pool_block = lax.dynamic_slice_in_dim(kv_pool, device * DEVICE_PAGES, DEVICE_PAGES, 0)
        table_block = lax.dynamic_slice_in_dim(block_table, device * RQ_DEV, RQ_DEV, 0)
        length_row = lax.dynamic_index_in_dim(context_len, device, 0, keepdims=False)
        return attend(query_block, fresh_block, pool_block, table_block, length_row)

    heads = lax.map(per_device, jnp.arange(PEER_DEVICES, dtype=jnp.int32))
    heads = jnp.transpose(heads, (1, 0, 2, 3)).reshape(DECODE_STEPS, DECODE_REQUESTS, QUERY_HEADS * HEAD_SIZE)

    def project(step_heads):
        return jnp.dot(step_heads, out_proj, preferred_element_type=jnp.float32).astype(jnp.bfloat16)

    decoded = lax.map(project, heads)
    ends = jnp.cumsum(prompt_blocks, 1).astype(jnp.int32)
    starts = (ends - prompt_blocks).astype(jnp.int32)
    local = jnp.arange(P_DEV, dtype=jnp.int32)
    inside = (local[None, :, None] >= starts[:, None, :]) & (local[None, :, None] < ends[:, None, :])

    def pick(table):
        return jnp.sum(jnp.where(inside, table[:, None, :], 0), 2).astype(jnp.int32)

    owner = pick(prompt_owner)
    slot = (local[None, :] - pick(starts)).astype(jnp.int32)
    last = local[None, :] == pick(ends) - 1
    valid = jnp.where(last, pick(prompt_tail), PAGE_TOKENS).astype(jnp.int32)
    source = jnp.arange(PEER_DEVICES, dtype=jnp.int32)[:, None]
    target_slot = (owner * (PEER_DEVICES * CAP) + source * CAP + slot).reshape(PROMPT_BLOCKS).astype(jnp.int32)
    keep = jnp.arange(PAGE_TOKENS, dtype=jnp.int32)[None, :] < valid.reshape(PROMPT_BLOCKS)[:, None]
    masked_scores = jnp.where(keep[:, :, None], finished_prompt_cache, jnp.zeros_like(finished_prompt_cache))
    migrated = jnp.zeros((RECEIVE_SLOTS, PAGE_TOKENS, KEY_VALUE_HEADS * 2 * HEAD_SIZE), jnp.bfloat16).at[target_slot].set(masked_scores)
    return (decoded, migrated)
```

```python
import jax
import jax.numpy as jnp
from jax import lax
from jax.experimental import pallas as pl
from jax.experimental.pallas import tpu as pltpu
from jax.sharding import PartitionSpec as P

HEAD_SIZE = 128
PAGE_TOKENS = 16
CAP = 3
NEGATIVE = -1e30
OFFSETS = (4, 3, -3, 2, -2, 1, -1, 0)
GROUP = 16


def attend_kernel(
    table_hbm,
    length_hbm,
    queries_hbm,
    fresh_hbm,
    pool_hbm,
    out,
    table,
    length,
    queries,
    fresh,
    pool,
    key_rows,
    value_rows,
    arrived,
):
    loads = [
        pltpu.make_async_copy(source, target, arrived.at[i])
        for i, (source, target) in enumerate(
            (
                (table_hbm, table),
                (length_hbm, length),
                (pool_hbm, pool),
                (fresh_hbm, fresh),
                (queries_hbm, queries),
            )
        )
    ]
    for load in loads:
        load.start()
    steps, rows, width = queries.shape
    heads = width // HEAD_SIZE
    pages = table.shape[0]
    context = pages * PAGE_TOKENS
    cached = GROUP * context
    recent = steps * GROUP
    scale = HEAD_SIZE ** (-0.5)

    def index(columns, axis):
        return lax.broadcasted_iota(jnp.int32, (GROUP, columns), axis)

    own_cached = index(cached, 1) // context == index(cached, 0)
    cached_place = index(cached, 1) % context
    own_recent = index(recent, 1) % GROUP == index(recent, 0)
    recent_bias = [
        jnp.where(own_recent & (index(recent, 1) // GROUP <= s), 0.0, NEGATIVE)
        for s in range(steps)
    ]
    tile_row = index(cached, 0)
    for load in loads:
        load.wait()
    for first in range(0, rows, GROUP):
        limit = jnp.zeros((GROUP, cached), jnp.int32)
        for r in range(GROUP):
            limit = jnp.where(tile_row == r, length[0, first + r], limit)
            for j in range(pages):
                page = pool[table[j, first + r]]
                at = pl.ds(r * context + j * PAGE_TOKENS, PAGE_TOKENS)
                key_rows[at, :] = page[:, :HEAD_SIZE]
                value_rows[at, :] = page[:, HEAD_SIZE:]
        for u in range(steps):
            token = fresh[u, pl.ds(first, GROUP), :]
            at = pl.ds(cached + u * GROUP, GROUP)
            key_rows[at, :] = token[:, :HEAD_SIZE]
            value_rows[at, :] = token[:, HEAD_SIZE:]
        cached_bias = jnp.where(own_cached & (cached_place < limit), 0.0, NEGATIVE)
        for s in range(steps):
            query = jnp.concatenate(
                [
                    queries[s, pl.ds(first, GROUP), h * HEAD_SIZE : (h + 1) * HEAD_SIZE]
                    for h in range(heads)
                ],
                0,
            )
            scores = lax.dot_general(
                query, key_rows[...], (((1,), (1,)), ((), ())), preferred_element_type=jnp.float32
            )
            bias = jnp.concatenate([cached_bias, recent_bias[s]], 1)
            scores = scores.reshape(heads, GROUP, cached + recent) * scale + bias[None]
            raw = jnp.exp(scores - jnp.max(scores, -1, keepdims=True))
            probs = (raw * (1.0 / jnp.sum(raw, -1, keepdims=True))).astype(jnp.bfloat16)
            mixed = jnp.dot(
                probs.reshape(heads * GROUP, cached + recent),
                value_rows[...],
                preferred_element_type=jnp.float32,
            ).astype(jnp.bfloat16)
            for h in range(heads):
                piece = mixed[h * GROUP : (h + 1) * GROUP]
                for copy in range(out.shape[0]):
                    out[copy, s, pl.ds(first, GROUP), h * HEAD_SIZE : (h + 1) * HEAD_SIZE] = piece


def attend(copies, queries, fresh, pool, table, length):
    steps, rows, width = queries.shape
    table = table.T
    keys = GROUP * (table.shape[0] * PAGE_TOKENS + steps)
    far = pl.BlockSpec(memory_space=pltpu.HBM)
    return pl.pallas_call(
        attend_kernel,
        out_shape=jax.ShapeDtypeStruct((copies, steps, rows, width), jnp.bfloat16),
        in_specs=[far] * 5,
        out_specs=pl.BlockSpec(memory_space=pltpu.VMEM),
        scratch_shapes=[
            pltpu.SMEM(table.shape, jnp.int32),
            pltpu.SMEM(length.shape, jnp.int32),
            pltpu.VMEM(queries.shape, queries.dtype),
            pltpu.VMEM(fresh.shape, fresh.dtype),
            pltpu.VMEM(pool.shape, pool.dtype),
            pltpu.VMEM((keys, HEAD_SIZE), jnp.bfloat16),
            pltpu.VMEM((keys, HEAD_SIZE), jnp.bfloat16),
            pltpu.SemaphoreType.DMA((5,)),
        ],
        compiler_params=pltpu.CompilerParams(vmem_limit_bytes=24 << 20),
        cost_estimate=pl.CostEstimate(
            flops=4 * steps * rows * (width // HEAD_SIZE) * keys * HEAD_SIZE,
            bytes_accessed=4 << 20,
            transcendentals=0,
        ),
        name="attend",
    )(table, length, queries, fresh, pool)


def pack_kernel(blocks, tail, owner, finished, out):
    out[...] = jnp.zeros_like(out)
    count = finished.shape[0]
    token = lax.broadcasted_iota(jnp.int32, finished.shape[1:], 0)

    def one(j, start):
        held = blocks[0, j]
        for slot in range(CAP):
            valid = jnp.where(slot == held - 1, tail[0, j], PAGE_TOKENS)
            valid = jnp.where(slot < held, valid, 0)
            block = finished[jnp.minimum(start + slot, count - 1)]
            out[owner[0, j] * CAP + slot] = jnp.where(token < valid, block, jnp.zeros_like(block))
        return start + held

    lax.fori_loop(0, blocks.shape[1], one, jnp.int32(0))


def pack(receivers, finished, blocks, tail, owner):
    smem = pl.BlockSpec(memory_space=pltpu.SMEM)
    vmem = pl.BlockSpec(memory_space=pltpu.VMEM)
    return pl.pallas_call(
        pack_kernel,
        out_shape=jax.ShapeDtypeStruct((receivers * CAP,) + finished.shape[1:], finished.dtype),
        in_specs=[smem, smem, smem, vmem],
        out_specs=vmem,
        compiler_params=pltpu.CompilerParams(vmem_limit_bytes=16 << 20),
        cost_estimate=pl.CostEstimate(flops=0, bytes_accessed=2 << 20, transcendentals=0),
        name="pack",
    )(blocks, tail, owner, finished)


def project_kernel(me, heads, weight, *outs):
    parts, steps, rows, width = heads.shape
    shares = len(OFFSETS)
    share = weight.shape[1] // shares
    lines = heads[...].reshape(parts * steps * rows, width)
    for at in range(0, shares, 2):
        columns = [
            weight[:, pl.ds(pl.multiple_of((me[0] + OFFSETS[at + i]) % shares * share, share), share)]
            for i in range(2)
        ]
        product = jnp.dot(
            lines, jnp.concatenate(columns, 1), preferred_element_type=jnp.float32
        ).astype(jnp.bfloat16)
        product = product.reshape(parts, steps, rows, 2 * share)
        for i in range(2):
            for q in range(parts):
                outs[at + i][:, q * rows : (q + 1) * rows, :] = product[
                    q, :, :, i * share : (i + 1) * share
                ]


def project(me, heads, weight):
    parts, steps, rows, width = heads.shape
    columns = weight.shape[1]
    share = columns // len(OFFSETS)
    vmem = pl.BlockSpec(memory_space=pltpu.VMEM)
    block = jax.ShapeDtypeStruct((steps, parts * rows, share), jnp.bfloat16)
    return pl.pallas_call(
        project_kernel,
        out_shape=[block] * len(OFFSETS),
        in_specs=[pl.BlockSpec(memory_space=pltpu.SMEM), vmem, vmem],
        out_specs=[vmem] * len(OFFSETS),
        compiler_params=pltpu.CompilerParams(vmem_limit_bytes=32 << 20),
        cost_estimate=pl.CostEstimate(
            flops=2 * parts * steps * rows * width * columns,
            bytes_accessed=6 << 20,
            transcendentals=0,
        ),
        name="project",
    )(me, heads, weight)


def sum_over_ring(blocks):
    size = lax.axis_size("tp")

    def shift(block, by):
        return lax.ppermute(block, "tp", [(i, (i + by) % size) for i in range(size)])

    def total(*terms):
        return sum(term.astype(jnp.float32) for term in terms)

    half = blocks[4].shape[0] // 2
    far_up = shift(blocks[4][:half], 2)
    far_down = shift(blocks[4][half:], -2)
    up, down = shift(blocks[3], 1), shift(blocks[-3], -1)
    near_up, near_down = shift(blocks[1], 1), shift(blocks[-1], -1)
    above = total(blocks[2], up)
    above = jnp.concatenate([above[:half] + far_up.astype(jnp.float32), above[half:]], 0)
    below = total(blocks[-2], down)
    below = jnp.concatenate([below[:half], below[half:] + far_down.astype(jnp.float32)], 0)
    above = shift(above.astype(jnp.bfloat16), 2)
    below = shift(below.astype(jnp.bfloat16), -2)
    return total(blocks[0], near_up, near_down, above, below).astype(jnp.bfloat16)


def per_device(
    queries,
    new_token_cache,
    kv_pool,
    block_table,
    context_len,
    out_proj,
    finished_prompt_cache,
    prompt_blocks,
    prompt_tail,
    prompt_owner,
):
    copies = lax.axis_size("seq")
    receivers = lax.axis_size("grp") * copies
    heads = attend(copies, queries, new_token_cache, kv_pool, block_table, context_len)
    gathered = lax.all_to_all(heads, "seq", split_axis=0, concat_axis=0, tiled=True)
    finished, _ = lax.optimization_barrier((finished_prompt_cache, heads))
    packed = pack(receivers, finished, prompt_blocks, prompt_tail, prompt_owner)
    packed, gathered = lax.optimization_barrier((packed, gathered))
    migrated = lax.all_to_all(packed, ("grp", "seq"), split_axis=0, concat_axis=0, tiled=True)
    me = lax.axis_index("tp").reshape(1)
    decoded = sum_over_ring(dict(zip(OFFSETS, project(me, gathered, out_proj))))
    return (decoded, migrated)


def solution(mesh):
    placed = (
        P(None, ("grp", "seq"), "tp"),
        P(None, ("grp", "seq"), "tp"),
        P(("grp", "seq"), None, "tp"),
        P(("grp", "seq"), None),
        P(("grp", "seq"), None),
        P("tp", "seq"),
        P(("grp", "seq"), None, "tp"),
        P(("grp", "seq"), None),
        P(("grp", "seq"), None),
        P(("grp", "seq"), None),
    )
    return jax.shard_map(
        per_device,
        mesh=mesh,
        in_specs=placed,
        out_specs=(P(None, "grp", ("seq", "tp")), P(("grp", "seq"), None, "tp")),
        check_vma=False,
    )
```

```python
import jax
import jax.numpy as jnp
from jax import lax
from jax.experimental import pallas as pl
from jax.experimental.pallas import tpu as pltpu
from jax.sharding import PartitionSpec as P

HEAD_SIZE = 128
PAGE_TOKENS = 16
CAP = 3
NEGATIVE = -1e30
OFFSETS = (4, 3, -3, 2, -2, 1, -1, 0)
PROJECT_WEIGHT = 10
GROUP = 16


def start_all(copies, arrived):
    started = [
        pltpu.make_async_copy(source, target, arrived.at[i])
        for i, (source, target) in enumerate(copies)
    ]
    for copy in started:
        copy.start()
    return started


def pack_blocks(blocks, tail, owner, finished, packed):
    count = finished.shape[0]
    token = lax.broadcasted_iota(jnp.int32, finished.shape[1:], 0)
    start = jnp.int32(0)
    for j in range(blocks.shape[1]):
        held = blocks[0, j]
        for slot in range(CAP):
            valid = jnp.where(slot == held - 1, tail[0, j], PAGE_TOKENS)
            valid = jnp.where(slot < held, valid, 0)
            block = finished[jnp.minimum(start + slot, count - 1)]
            packed[owner[0, j] * CAP + slot] = jnp.where(
                token < valid, block, jnp.zeros_like(block)
            )
        start = start + held


def attend_kernel(
    blocks_hbm,
    tail_hbm,
    owner_hbm,
    finished_hbm,
    table_hbm,
    length_hbm,
    pool_hbm,
    fresh_hbm,
    queries_hbm,
    out,
    packed_hbm,
    blocks,
    tail,
    owner,
    finished,
    table,
    length,
    pool,
    fresh,
    queries,
    packed,
    key_rows,
    value_rows,
    arrived,
    left,
):
    sources = (blocks_hbm, tail_hbm, owner_hbm, finished_hbm)
    sources += (table_hbm, length_hbm, pool_hbm, fresh_hbm, queries_hbm)
    targets = (blocks, tail, owner, finished, table, length, pool, fresh, queries)
    loads = start_all(list(zip(sources, targets)), arrived)
    packed[...] = jnp.zeros_like(packed)
    steps, rows, width = queries.shape
    heads = width // HEAD_SIZE
    pages = table.shape[0]
    context = pages * PAGE_TOKENS
    cached = GROUP * context
    recent = steps * GROUP
    scale = HEAD_SIZE ** (-0.5)

    def index(columns, axis):
        return lax.broadcasted_iota(jnp.int32, (GROUP, columns), axis)

    own_cached = index(cached, 1) // context == index(cached, 0)
    cached_place = index(cached, 1) % context
    own_recent = index(recent, 1) % GROUP == index(recent, 0)
    recent_bias = [
        jnp.where(own_recent & (index(recent, 1) // GROUP <= s), 0.0, NEGATIVE)
        for s in range(steps)
    ]
    tile_row = index(cached, 0)
    for load in loads:
        load.wait()
    pack_blocks(blocks, tail, owner, finished, packed)
    (store,) = start_all([(packed, packed_hbm)], left)
    groups = range(rows // GROUP)
    cached_bias = []
    for g in groups:
        first = g * GROUP
        limit = jnp.zeros((GROUP, cached), jnp.int32)
        for r in range(GROUP):
            limit = jnp.where(tile_row == r, length[0, first + r], limit)
            for j in range(pages):
                page = pool[table[j, first + r]]
                at = pl.ds(r * context + j * PAGE_TOKENS, PAGE_TOKENS)
                key_rows[g, at, :] = page[:, :HEAD_SIZE]
                value_rows[g, at, :] = page[:, HEAD_SIZE:]
        for u in range(steps):
            token = fresh[u, pl.ds(first, GROUP), :]
            at = pl.ds(cached + u * GROUP, GROUP)
            key_rows[g, at, :] = token[:, :HEAD_SIZE]
            value_rows[g, at, :] = token[:, HEAD_SIZE:]
        cached_bias.append(jnp.where(own_cached & (cached_place < limit), 0.0, NEGATIVE))
    for g in groups:
        at = pl.ds(g * GROUP, GROUP)
        scores = []
        for s in range(steps):
            query = jnp.concatenate(
                [queries[s, at, h * HEAD_SIZE : (h + 1) * HEAD_SIZE] for h in range(heads)], 0
            )
            scores.append(
                lax.dot_general(
                    query,
                    key_rows[g],
                    (((1,), (1,)), ((), ())),
                    preferred_element_type=jnp.float32,
                )
            )
        probs = []
        for s in range(steps):
            bias = jnp.concatenate([cached_bias[g], recent_bias[s]], 1)
            masked = scores[s].reshape(heads, GROUP, cached + recent) * scale + bias[None]
            raw = jnp.exp(masked - jnp.max(masked, -1, keepdims=True))
            share = raw * (1.0 / jnp.sum(raw, -1, keepdims=True))
            probs.append(share.astype(jnp.bfloat16).reshape(heads * GROUP, cached + recent))
        for s in range(steps):
            mixed = jnp.dot(probs[s], value_rows[g], preferred_element_type=jnp.float32)
            mixed = mixed.astype(jnp.bfloat16)
            for h in range(heads):
                out[s, at, h * HEAD_SIZE : (h + 1) * HEAD_SIZE] = mixed[h * GROUP : (h + 1) * GROUP]
    store.wait()


def attend_and_pack(receivers, queries, fresh, pool, table, length, finished, blocks, tail, owner):
    steps, rows, width = queries.shape
    table = table.T
    keys = GROUP * (table.shape[0] * PAGE_TOKENS + steps)
    operands = (blocks, tail, owner, finished, table, length, pool, fresh, queries)
    far = pl.BlockSpec(memory_space=pltpu.HBM)
    packed = (receivers * CAP,) + finished.shape[1:]
    return pl.pallas_call(
        attend_kernel,
        out_shape=[
            jax.ShapeDtypeStruct(queries.shape, jnp.bfloat16),
            jax.ShapeDtypeStruct(packed, finished.dtype),
        ],
        in_specs=[far] * len(operands),
        out_specs=[pl.BlockSpec(memory_space=pltpu.VMEM), far],
        scratch_shapes=[
            pltpu.SMEM(operand.shape, operand.dtype)
            if operand.dtype == jnp.int32
            else pltpu.VMEM(operand.shape, operand.dtype)
            for operand in operands
        ]
        + [
            pltpu.VMEM(packed, finished.dtype),
            pltpu.VMEM((rows // GROUP, keys, HEAD_SIZE), jnp.bfloat16),
            pltpu.VMEM((rows // GROUP, keys, HEAD_SIZE), jnp.bfloat16),
            pltpu.SemaphoreType.DMA((len(operands),)),
            pltpu.SemaphoreType.DMA((1,)),
        ],
        compiler_params=pltpu.CompilerParams(vmem_limit_bytes=60 << 20),
        cost_estimate=pl.CostEstimate(
            flops=4 * steps * rows * (width // HEAD_SIZE) * keys * HEAD_SIZE,
            bytes_accessed=5 << 20,
            transcendentals=0,
        ),
        name="attend_and_pack",
    )(*operands)


def project_kernel(me, place, *refs):
    parts = refs[: -1 - len(OFFSETS)]
    weight = refs[len(parts)]
    outs = refs[len(parts) + 1 :]
    steps, rows, width = parts[0].shape
    shares = len(OFFSETS)
    share = weight.shape[1] // shares
    lines = jnp.concatenate([part[...].reshape(steps * rows, width) for part in parts], 0)
    for at in range(0, shares, 2):
        columns = [
            weight[:, pl.ds(pl.multiple_of((me[0] + OFFSETS[at + i]) % shares * share, share), share)]
            for i in range(2)
        ]
        product = jnp.dot(
            lines, jnp.concatenate(columns, 1), preferred_element_type=jnp.float32
        ).astype(jnp.bfloat16)
        product = product.reshape(len(parts), steps, rows, 2 * share)
        for q in range(len(parts)):
            to = pl.ds(pl.multiple_of(place[q] * rows, rows), rows)
            for i in range(2):
                outs[at + i][:, to, :] = product[q, :, :, i * share : (i + 1) * share]


def project(me, place, parts, weight):
    steps, rows, width = parts[0].shape
    columns = weight.shape[1]
    share = columns // len(OFFSETS)
    smem = pl.BlockSpec(memory_space=pltpu.SMEM)
    vmem = pl.BlockSpec(memory_space=pltpu.VMEM)
    block = jax.ShapeDtypeStruct((steps, len(parts) * rows, share), jnp.bfloat16)
    return pl.pallas_call(
        project_kernel,
        out_shape=[block] * len(OFFSETS),
        in_specs=[smem, smem] + [vmem] * (len(parts) + 1),
        out_specs=[vmem] * len(OFFSETS),
        compiler_params=pltpu.CompilerParams(vmem_limit_bytes=32 << 20),
        cost_estimate=pl.CostEstimate(
            flops=PROJECT_WEIGHT * 2 * len(parts) * steps * rows * width * columns,
            bytes_accessed=6 << 20,
            transcendentals=0,
        ),
        name="project",
    )(me, place, *parts, weight)


def gather_heads(heads):
    across, along = 2, lax.axis_size("seq") // 2

    def shift(block, by):
        pairs = [(z * along + x, z * along + (x + by) % along) for z in range(across) for x in range(along)]
        return lax.ppermute(block, "seq", pairs)

    me = lax.axis_index("seq")
    z, x = me // along, me % along
    other = lax.ppermute(heads, "seq", [(i, (i + along) % (2 * along)) for i in range(2 * along)])
    parts, place = [heads, other], [me, (1 - z) * along + x]
    for row, block in ((z, heads), (1 - z, other)):
        for by in (1, -1, 2):
            parts.append(shift(block, by))
            place.append(row * along + (x - by) % along)
    return parts, jnp.stack(place)


def finish_kernel(migrated_hbm, *refs):
    terms, (out, moved_hbm, moved) = refs[:-3], refs[-3:]
    copy = pltpu.make_async_copy(migrated_hbm, moved_hbm, moved)
    copy.start()
    out[...] = sum(term[...].astype(jnp.float32) for term in terms).astype(out.dtype)
    copy.wait()


def finish(migrated, terms):
    far = pl.BlockSpec(memory_space=pltpu.HBM)
    vmem = pl.BlockSpec(memory_space=pltpu.VMEM)
    return pl.pallas_call(
        finish_kernel,
        out_shape=[
            jax.ShapeDtypeStruct(terms[0].shape, jnp.bfloat16),
            jax.ShapeDtypeStruct(migrated.shape, migrated.dtype),
        ],
        in_specs=[far] + [vmem] * len(terms),
        out_specs=[vmem, far],
        scratch_shapes=[pltpu.SemaphoreType.DMA],
        compiler_params=pltpu.CompilerParams(vmem_limit_bytes=32 << 20),
        cost_estimate=pl.CostEstimate(flops=0, bytes_accessed=4 << 20, transcendentals=0),
        name="finish",
    )(migrated, *terms)


def signs(me):
    return 1 - 2 * (me % 2), 1 - 2 * (me // 2 % 2)


def share_order(me):
    near, next_near = signs(me)
    offsets = (4, 3 * near, -3 * near, 2 * next_near, -2 * next_near, near, -near, 0)
    return jnp.stack([(me + offset) % SHARES for offset in offsets])


def send_round_ring(blocks):
    size = lax.axis_size("tp")

    def shift(block, by):
        return lax.ppermute(block, "tp", [(i, (i + by) % size) for i in range(size)])

    def total(*terms):
        return sum(term.astype(jnp.float32) for term in terms)

    half = blocks[4].shape[0] // 2
    far_up = shift(blocks[4][:half], 2)
    far_down = shift(blocks[4][half:], -2)
    up, down = shift(blocks[3], 1), shift(blocks[-3], -1)
    near_up, near_down = shift(blocks[1], 1), shift(blocks[-1], -1)
    above = total(blocks[2], up)
    above = jnp.concatenate([above[:half] + far_up.astype(jnp.float32), above[half:]], 0)
    below = total(blocks[-2], down)
    below = jnp.concatenate([below[:half], below[half:] + far_down.astype(jnp.float32)], 0)
    above = shift(above.astype(jnp.bfloat16), 2)
    below = shift(below.astype(jnp.bfloat16), -2)
    return blocks[0], near_up, near_down, above, below


def per_device(
    queries,
    new_token_cache,
    kv_pool,
    block_table,
    context_len,
    out_proj,
    finished_prompt_cache,
    prompt_blocks,
    prompt_tail,
    prompt_owner,
):
    receivers = lax.axis_size("grp") * lax.axis_size("seq")
    heads, packed = attend_and_pack(
        receivers,
        queries,
        new_token_cache,
        kv_pool,
        block_table,
        context_len,
        finished_prompt_cache,
        prompt_blocks,
        prompt_tail,
        prompt_owner,
    )
    parts, place = gather_heads(heads)
    migrated = lax.all_to_all(packed, ("grp", "seq"), split_axis=0, concat_axis=0, tiled=True)
    me = lax.axis_index("tp").reshape(1)
    terms = send_round_ring(dict(zip(OFFSETS, project(me, place, parts, out_proj))))
    decoded, migrated = finish(migrated, terms)
    return (decoded, migrated)


def solution(mesh):
    placed = (
        P(None, ("grp", "seq"), "tp"),
        P(None, ("grp", "seq"), "tp"),
        P(("grp", "seq"), None, "tp"),
        P(("grp", "seq"), None),
        P(("grp", "seq"), None),
        P("tp", "seq"),
        P(("grp", "seq"), None, "tp"),
        P(("grp", "seq"), None),
        P(("grp", "seq"), None),
        P(("grp", "seq"), None),
    )
    return jax.shard_map(
        per_device,
        mesh=mesh,
        in_specs=placed,
        out_specs=(P(None, "grp", ("seq", "tp")), P(("grp", "seq"), None, "tp")),
        check_vma=False,
    )
```

```python
import jax
import jax.numpy as jnp
from jax import lax
from jax.experimental import pallas as pl
from jax.experimental.pallas import tpu as pltpu
from jax.sharding import PartitionSpec as P

HEAD_SIZE = 128
PAGE_TOKENS = 16
CAP = 3
NEGATIVE = -1e30
OFFSETS = (4, 3, -3, 2, -2, 1, -1, 0)
PROJECT_WEIGHT = 10
GROUP = 16


def start_all(copies, arrived):
    started = [
        pltpu.make_async_copy(source, target, arrived.at[i])
        for i, (source, target) in enumerate(copies)
    ]
    for copy in started:
        copy.start()
    return started


def pack_blocks(blocks, tail, owner, finished, packed):
    count = finished.shape[0]
    token = lax.broadcasted_iota(jnp.int32, finished.shape[1:], 0)
    start = jnp.int32(0)
    for j in range(blocks.shape[1]):
        held = blocks[0, j]
        for slot in range(CAP):
            valid = jnp.where(slot == held - 1, tail[0, j], PAGE_TOKENS)
            valid = jnp.where(slot < held, valid, 0)
            block = finished[jnp.minimum(start + slot, count - 1)]
            packed[owner[0, j] * CAP + slot] = jnp.where(
                token < valid, block, jnp.zeros_like(block)
            )
        start = start + held


def attend_kernel(
    blocks_hbm,
    tail_hbm,
    owner_hbm,
    finished_hbm,
    table_hbm,
    length_hbm,
    pool_hbm,
    fresh_hbm,
    queries_hbm,
    out,
    packed_hbm,
    blocks,
    tail,
    owner,
    finished,
    table,
    length,
    pool,
    fresh,
    queries,
    packed,
    key_rows,
    value_rows,
    arrived,
    left,
):
    sources = (blocks_hbm, tail_hbm, owner_hbm, finished_hbm)
    sources += (table_hbm, length_hbm, pool_hbm, fresh_hbm, queries_hbm)
    targets = (blocks, tail, owner, finished, table, length, pool, fresh, queries)
    loads = start_all(list(zip(sources, targets)), arrived)
    packed[...] = jnp.zeros_like(packed)
    steps, rows, width = queries.shape
    heads = width // HEAD_SIZE
    pages = table.shape[0]
    context = pages * PAGE_TOKENS
    cached = GROUP * context
    recent = steps * GROUP
    scale = HEAD_SIZE ** (-0.5)

    def index(columns, axis):
        return lax.broadcasted_iota(jnp.int32, (GROUP, columns), axis)

    own_cached = index(cached, 1) // context == index(cached, 0)
    cached_place = index(cached, 1) % context
    own_recent = index(recent, 1) % GROUP == index(recent, 0)
    recent_bias = [
        jnp.where(own_recent & (index(recent, 1) // GROUP <= s), 0.0, NEGATIVE)
        for s in range(steps)
    ]
    tile_row = index(cached, 0)
    for load in loads:
        load.wait()
    pack_blocks(blocks, tail, owner, finished, packed)
    (store,) = start_all([(packed, packed_hbm)], left)
    groups = range(rows // GROUP)
    cached_bias = []
    for g in groups:
        first = g * GROUP
        limit = jnp.zeros((GROUP, cached), jnp.int32)
        for r in range(GROUP):
            limit = jnp.where(tile_row == r, length[0, first + r], limit)
            for j in range(pages):
                page = pool[table[j, first + r]]
                at = pl.ds(r * context + j * PAGE_TOKENS, PAGE_TOKENS)
                key_rows[g, at, :] = page[:, :HEAD_SIZE]
                value_rows[g, at, :] = page[:, HEAD_SIZE:]
        for u in range(steps):
            token = fresh[u, pl.ds(first, GROUP), :]
            at = pl.ds(cached + u * GROUP, GROUP)
            key_rows[g, at, :] = token[:, :HEAD_SIZE]
            value_rows[g, at, :] = token[:, HEAD_SIZE:]
        cached_bias.append(jnp.where(own_cached & (cached_place < limit), 0.0, NEGATIVE))
    for g in groups:
        at = pl.ds(g * GROUP, GROUP)
        scores = []
        for s in range(steps):
            query = jnp.concatenate(
                [queries[s, at, h * HEAD_SIZE : (h + 1) * HEAD_SIZE] for h in range(heads)], 0
            )
            scores.append(
                lax.dot_general(
                    query,
                    key_rows[g],
                    (((1,), (1,)), ((), ())),
                    preferred_element_type=jnp.float32,
                )
            )
        probs = []
        for s in range(steps):
            bias = jnp.concatenate([cached_bias[g], recent_bias[s]], 1)
            masked = scores[s].reshape(heads, GROUP, cached + recent) * scale + bias[None]
            raw = jnp.exp(masked - jnp.max(masked, -1, keepdims=True))
            share = raw * (1.0 / jnp.sum(raw, -1, keepdims=True))
            probs.append(share.astype(jnp.bfloat16).reshape(heads * GROUP, cached + recent))
        for s in range(steps):
            mixed = jnp.dot(probs[s], value_rows[g], preferred_element_type=jnp.float32)
            mixed = mixed.astype(jnp.bfloat16)
            for h in range(heads):
                out[s, at, h * HEAD_SIZE : (h + 1) * HEAD_SIZE] = mixed[h * GROUP : (h + 1) * GROUP]
    store.wait()


def attend_and_pack(receivers, queries, fresh, pool, table, length, finished, blocks, tail, owner):
    steps, rows, width = queries.shape
    table = table.T
    keys = GROUP * (table.shape[0] * PAGE_TOKENS + steps)
    operands = (blocks, tail, owner, finished, table, length, pool, fresh, queries)
    far = pl.BlockSpec(memory_space=pltpu.HBM)
    packed = (receivers * CAP,) + finished.shape[1:]
    return pl.pallas_call(
        attend_kernel,
        out_shape=[
            jax.ShapeDtypeStruct(queries.shape, jnp.bfloat16),
            jax.ShapeDtypeStruct(packed, finished.dtype),
        ],
        in_specs=[far] * len(operands),
        out_specs=[pl.BlockSpec(memory_space=pltpu.VMEM), far],
        scratch_shapes=[
            pltpu.SMEM(operand.shape, operand.dtype)
            if operand.dtype == jnp.int32
            else pltpu.VMEM(operand.shape, operand.dtype)
            for operand in operands
        ]
        + [
            pltpu.VMEM(packed, finished.dtype),
            pltpu.VMEM((rows // GROUP, keys, HEAD_SIZE), jnp.bfloat16),
            pltpu.VMEM((rows // GROUP, keys, HEAD_SIZE), jnp.bfloat16),
            pltpu.SemaphoreType.DMA((len(operands),)),
            pltpu.SemaphoreType.DMA((1,)),
        ],
        compiler_params=pltpu.CompilerParams(vmem_limit_bytes=60 << 20),
        cost_estimate=pl.CostEstimate(
            flops=4 * steps * rows * (width // HEAD_SIZE) * keys * HEAD_SIZE,
            bytes_accessed=5 << 20,
            transcendentals=0,
        ),
        name="attend_and_pack",
    )(*operands)


def project_kernel(me, place, *refs):
    parts = refs[: -1 - len(OFFSETS)]
    weight = refs[len(parts)]
    outs = refs[len(parts) + 1 :]
    steps, rows, width = parts[0].shape
    shares = len(OFFSETS)
    share = weight.shape[1] // shares
    lines = jnp.concatenate([part[...].reshape(steps * rows, width) for part in parts], 0)
    for at in range(0, shares, 2):
        columns = [
            weight[:, pl.ds(pl.multiple_of((me[0] + OFFSETS[at + i]) % shares * share, share), share)]
            for i in range(2)
        ]
        product = jnp.dot(
            lines, jnp.concatenate(columns, 1), preferred_element_type=jnp.float32
        ).astype(jnp.bfloat16)
        product = product.reshape(len(parts), steps, rows, 2 * share)
        for q in range(len(parts)):
            to = pl.ds(pl.multiple_of(place[q] * rows, rows), rows)
            for i in range(2):
                outs[at + i][:, to, :] = product[q, :, :, i * share : (i + 1) * share]


def project(me, place, parts, weight):
    steps, rows, width = parts[0].shape
    columns = weight.shape[1]
    share = columns // len(OFFSETS)
    smem = pl.BlockSpec(memory_space=pltpu.SMEM)
    vmem = pl.BlockSpec(memory_space=pltpu.VMEM)
    block = jax.ShapeDtypeStruct((steps, len(parts) * rows, share), jnp.bfloat16)
    return pl.pallas_call(
        project_kernel,
        out_shape=[block] * len(OFFSETS),
        in_specs=[smem, smem] + [vmem] * (len(parts) + 1),
        out_specs=[vmem] * len(OFFSETS),
        compiler_params=pltpu.CompilerParams(vmem_limit_bytes=32 << 20),
        cost_estimate=pl.CostEstimate(
            flops=PROJECT_WEIGHT * 2 * len(parts) * steps * rows * width * columns,
            bytes_accessed=6 << 20,
            transcendentals=0,
        ),
        name="project",
    )(me, place, *parts, weight)


def gather_heads(heads):
    across, along = 2, lax.axis_size("seq") // 2

    def shift(block, by):
        pairs = [(z * along + x, z * along + (x + by) % along) for z in range(across) for x in range(along)]
        return lax.ppermute(block, "seq", pairs)

    me = lax.axis_index("seq")
    z, x = me // along, me % along
    other = lax.ppermute(heads, "seq", [(i, (i + along) % (2 * along)) for i in range(2 * along)])
    parts, place = [heads, other], [me, (1 - z) * along + x]
    for row, block in ((z, heads), (1 - z, other)):
        for by in (1, -1, 2):
            parts.append(shift(block, by))
            place.append(row * along + (x - by) % along)
    return parts, jnp.stack(place)


def move_kernel(source, target, held, arrived, left):
    parts = arrived.shape[0]
    rows = held.shape[0] // parts
    spans = [pl.ds(i * rows, rows) for i in range(parts)]
    loads = start_all([(source.at[span], held.at[span]) for span in spans], arrived)
    stores = []
    for i, span in enumerate(spans):
        loads[i].wait()
        stores += start_all([(held.at[span], target.at[span])], left.at[pl.ds(i, 1)])
    for store in stores:
        store.wait()


def move(migrated):
    far = pl.BlockSpec(memory_space=pltpu.HBM)
    return pl.pallas_call(
        move_kernel,
        out_shape=jax.ShapeDtypeStruct(migrated.shape, migrated.dtype),
        in_specs=[far],
        out_specs=far,
        scratch_shapes=[
            pltpu.VMEM(migrated.shape, migrated.dtype),
            pltpu.SemaphoreType.DMA((4,)),
            pltpu.SemaphoreType.DMA((4,)),
        ],
        compiler_params=pltpu.CompilerParams(vmem_limit_bytes=60 << 20),
        cost_estimate=pl.CostEstimate(flops=0, bytes_accessed=3 << 20, transcendentals=0),
        name="move",
    )(migrated)


def send_round_ring(blocks):
    size = lax.axis_size("tp")

    def shift(block, by):
        return lax.ppermute(block, "tp", [(i, (i + by) % size) for i in range(size)])

    def total(*terms):
        return sum(term.astype(jnp.float32) for term in terms)

    half = blocks[4].shape[0] // 2
    far_up = shift(blocks[4][:half], 2)
    far_down = shift(blocks[4][half:], -2)
    up, near_up = shift(jnp.stack([blocks[3], blocks[1]]), 1)
    down, near_down = shift(jnp.stack([blocks[-3], blocks[-1]]), -1)
    above = total(blocks[2], up)
    above = jnp.concatenate([above[:half] + far_up.astype(jnp.float32), above[half:]], 0)
    below = total(blocks[-2], down)
    below = jnp.concatenate([below[:half], below[half:] + far_down.astype(jnp.float32)], 0)
    above = shift(above.astype(jnp.bfloat16), 2)
    below = shift(below.astype(jnp.bfloat16), -2)
    return blocks[0], near_up, near_down, above, below


def per_device(
    queries,
    new_token_cache,
    kv_pool,
    block_table,
    context_len,
    out_proj,
    finished_prompt_cache,
    prompt_blocks,
    prompt_tail,
    prompt_owner,
):
    receivers = lax.axis_size("grp") * lax.axis_size("seq")
    heads, packed = attend_and_pack(
        receivers,
        queries,
        new_token_cache,
        kv_pool,
        block_table,
        context_len,
        finished_prompt_cache,
        prompt_blocks,
        prompt_tail,
        prompt_owner,
    )
    parts, place = gather_heads(heads)
    migrated = lax.all_to_all(packed, ("grp", "seq"), split_axis=0, concat_axis=0, tiled=True)
    me = lax.axis_index("tp").reshape(1)
    terms = send_round_ring(dict(zip(OFFSETS, project(me, place, parts, out_proj))))
    migrated = move(migrated)
    migrated, own = lax.optimization_barrier((migrated, terms[0]))
    terms = (own,) + terms[1:]
    decoded = sum(term.astype(jnp.float32) for term in terms).astype(jnp.bfloat16)
    return (decoded, migrated)


def solution(mesh):
    placed = (
        P(None, ("grp", "seq"), "tp"),
        P(None, ("grp", "seq"), "tp"),
        P(("grp", "seq"), None, "tp"),
        P(("grp", "seq"), None),
        P(("grp", "seq"), None),
        P("tp", "seq"),
        P(("grp", "seq"), None, "tp"),
        P(("grp", "seq"), None),
        P(("grp", "seq"), None),
        P(("grp", "seq"), None),
    )
    return jax.shard_map(
        per_device,
        mesh=mesh,
        in_specs=placed,
        out_specs=(P(None, "grp", ("seq", "tp")), P(("grp", "seq"), None, "tp")),
        check_vma=False,
    )
```

```python
import jax
import jax.numpy as jnp
from jax import lax
from jax.experimental import pallas as pl
from jax.experimental.pallas import tpu as pltpu
from jax.sharding import PartitionSpec as P

HEAD_SIZE = 128
PAGE_TOKENS = 16
CAP = 3
NEGATIVE = -1e30
OFFSETS = (4, 3, -3, 2, -2, 1, -1, 0)
PROJECT_WEIGHT = 10
GROUP = 16


def start_all(copies, arrived):
    started = [
        pltpu.make_async_copy(source, target, arrived.at[i])
        for i, (source, target) in enumerate(copies)
    ]
    for copy in started:
        copy.start()
    return started


def pack_blocks(blocks, tail, owner, finished, packed):
    count = finished.shape[0]
    token = lax.broadcasted_iota(jnp.int32, finished.shape[1:], 0)
    start = jnp.int32(0)
    for j in range(blocks.shape[1]):
        held = blocks[0, j]
        for slot in range(CAP):
            valid = jnp.where(slot == held - 1, tail[0, j], PAGE_TOKENS)
            valid = jnp.where(slot < held, valid, 0)
            block = finished[jnp.minimum(start + slot, count - 1)]
            packed[owner[0, j] * CAP + slot] = jnp.where(
                token < valid, block, jnp.zeros_like(block)
            )
        start = start + held


def attend_kernel(
    blocks_hbm,
    tail_hbm,
    owner_hbm,
    finished_hbm,
    table_hbm,
    length_hbm,
    pool_hbm,
    fresh_hbm,
    queries_hbm,
    out,
    packed_hbm,
    blocks,
    tail,
    owner,
    finished,
    table,
    length,
    pool,
    fresh,
    queries,
    packed,
    key_rows,
    value_rows,
    arrived,
    left,
):
    sources = (blocks_hbm, tail_hbm, owner_hbm, finished_hbm)
    sources += (table_hbm, length_hbm, pool_hbm, fresh_hbm, queries_hbm)
    targets = (blocks, tail, owner, finished, table, length, pool, fresh, queries)
    loads = start_all(list(zip(sources, targets)), arrived)
    packed[...] = jnp.zeros_like(packed)
    steps, rows, width = queries.shape
    heads = width // HEAD_SIZE
    pages = table.shape[0]
    context = pages * PAGE_TOKENS
    cached = GROUP * context
    recent = steps * GROUP
    scale = HEAD_SIZE ** (-0.5)

    def index(columns, axis):
        return lax.broadcasted_iota(jnp.int32, (GROUP, columns), axis)

    own_cached = index(cached, 1) // context == index(cached, 0)
    cached_place = index(cached, 1) % context
    own_recent = index(recent, 1) % GROUP == index(recent, 0)
    recent_bias = [
        jnp.where(own_recent & (index(recent, 1) // GROUP <= s), 0.0, NEGATIVE)
        for s in range(steps)
    ]
    tile_row = index(cached, 0)
    for load in loads[:4]:
        load.wait()
    pack_blocks(blocks, tail, owner, finished, packed)
    (store,) = start_all([(packed, packed_hbm)], left)
    for load in loads[4:]:
        load.wait()
    groups = range(rows // GROUP)
    cached_bias = []
    for g in groups:
        first = g * GROUP
        limit = jnp.zeros((GROUP, cached), jnp.int32)
        for r in range(GROUP):
            limit = jnp.where(tile_row == r, length[0, first + r], limit)
            for j in range(pages):
                page = pool[table[j, first + r]]
                at = pl.ds(r * context + j * PAGE_TOKENS, PAGE_TOKENS)
                key_rows[g, at, :] = page[:, :HEAD_SIZE]
                value_rows[g, at, :] = page[:, HEAD_SIZE:]
        for u in range(steps):
            token = fresh[u, pl.ds(first, GROUP), :]
            at = pl.ds(cached + u * GROUP, GROUP)
            key_rows[g, at, :] = token[:, :HEAD_SIZE]
            value_rows[g, at, :] = token[:, HEAD_SIZE:]
        cached_bias.append(jnp.where(own_cached & (cached_place < limit), 0.0, NEGATIVE))
    for g in groups:
        at = pl.ds(g * GROUP, GROUP)
        scores = []
        for s in range(steps):
            query = jnp.concatenate(
                [queries[s, at, h * HEAD_SIZE : (h + 1) * HEAD_SIZE] for h in range(heads)], 0
            )
            scores.append(
                lax.dot_general(
                    query,
                    key_rows[g],
                    (((1,), (1,)), ((), ())),
                    preferred_element_type=jnp.float32,
                )
            )
        probs = []
        for s in range(steps):
            bias = jnp.concatenate([cached_bias[g], recent_bias[s]], 1)
            masked = scores[s].reshape(heads, GROUP, cached + recent) * scale + bias[None]
            raw = jnp.exp(masked - jnp.max(masked, -1, keepdims=True))
            share = raw * (1.0 / jnp.sum(raw, -1, keepdims=True))
            probs.append(share.astype(jnp.bfloat16).reshape(heads * GROUP, cached + recent))
        for s in range(steps):
            mixed = jnp.dot(probs[s], value_rows[g], preferred_element_type=jnp.float32)
            mixed = mixed.astype(jnp.bfloat16)
            for h in range(heads):
                out[s, at, h * HEAD_SIZE : (h + 1) * HEAD_SIZE] = mixed[h * GROUP : (h + 1) * GROUP]
    store.wait()


def attend_and_pack(receivers, queries, fresh, pool, table, length, finished, blocks, tail, owner):
    steps, rows, width = queries.shape
    table = table.T
    keys = GROUP * (table.shape[0] * PAGE_TOKENS + steps)
    operands = (blocks, tail, owner, finished, table, length, pool, fresh, queries)
    far = pl.BlockSpec(memory_space=pltpu.HBM)
    packed = (receivers * CAP,) + finished.shape[1:]
    return pl.pallas_call(
        attend_kernel,
        out_shape=[
            jax.ShapeDtypeStruct(queries.shape, jnp.bfloat16),
            jax.ShapeDtypeStruct(packed, finished.dtype),
        ],
        in_specs=[far] * len(operands),
        out_specs=[pl.BlockSpec(memory_space=pltpu.VMEM), far],
        scratch_shapes=[
            pltpu.SMEM(operand.shape, operand.dtype)
            if operand.dtype == jnp.int32
            else pltpu.VMEM(operand.shape, operand.dtype)
            for operand in operands
        ]
        + [
            pltpu.VMEM(packed, finished.dtype),
            pltpu.VMEM((rows // GROUP, keys, HEAD_SIZE), jnp.bfloat16),
            pltpu.VMEM((rows // GROUP, keys, HEAD_SIZE), jnp.bfloat16),
            pltpu.SemaphoreType.DMA((len(operands),)),
            pltpu.SemaphoreType.DMA((1,)),
        ],
        compiler_params=pltpu.CompilerParams(vmem_limit_bytes=60 << 20),
        cost_estimate=pl.CostEstimate(
            flops=4 * steps * rows * (width // HEAD_SIZE) * keys * HEAD_SIZE,
            bytes_accessed=5 << 20,
            transcendentals=0,
        ),
        name="attend_and_pack",
    )(*operands)


def project_kernel(me, place, *refs):
    parts = refs[: -1 - len(OFFSETS)]
    weight = refs[len(parts)]
    outs = refs[len(parts) + 1 :]
    steps, rows, width = parts[0].shape
    shares = len(OFFSETS)
    share = weight.shape[1] // shares
    lines = jnp.concatenate([part[...].reshape(steps * rows, width) for part in parts], 0)
    for at in range(0, shares, 2):
        columns = [
            weight[:, pl.ds(pl.multiple_of((me[0] + OFFSETS[at + i]) % shares * share, share), share)]
            for i in range(2)
        ]
        product = jnp.dot(
            lines, jnp.concatenate(columns, 1), preferred_element_type=jnp.float32
        ).astype(jnp.bfloat16)
        product = product.reshape(len(parts), steps, rows, 2 * share)
        for q in range(len(parts)):
            to = pl.ds(pl.multiple_of(place[q] * rows, rows), rows)
            for i in range(2):
                outs[at + i][:, to, :] = product[q, :, :, i * share : (i + 1) * share]


def project(me, place, parts, weight):
    steps, rows, width = parts[0].shape
    columns = weight.shape[1]
    share = columns // len(OFFSETS)
    smem = pl.BlockSpec(memory_space=pltpu.SMEM)
    vmem = pl.BlockSpec(memory_space=pltpu.VMEM)
    block = jax.ShapeDtypeStruct((steps, len(parts) * rows, share), jnp.bfloat16)
    return pl.pallas_call(
        project_kernel,
        out_shape=[block] * len(OFFSETS),
        in_specs=[smem, smem] + [vmem] * (len(parts) + 1),
        out_specs=[vmem] * len(OFFSETS),
        compiler_params=pltpu.CompilerParams(vmem_limit_bytes=32 << 20),
        cost_estimate=pl.CostEstimate(
            flops=PROJECT_WEIGHT * 2 * len(parts) * steps * rows * width * columns,
            bytes_accessed=6 << 20,
            transcendentals=0,
        ),
        name="project",
    )(me, place, *parts, weight)


def gather_heads(heads):
    across, along = 2, lax.axis_size("seq") // 2

    def shift(block, by):
        pairs = [(z * along + x, z * along + (x + by) % along) for z in range(across) for x in range(along)]
        return lax.ppermute(block, "seq", pairs)

    me = lax.axis_index("seq")
    z, x = me // along, me % along
    other = lax.ppermute(heads, "seq", [(i, (i + along) % (2 * along)) for i in range(2 * along)])
    parts, place = [heads, other], [me, (1 - z) * along + x]
    for row, block in ((z, heads), (1 - z, other)):
        for by in (1, -1, 2):
            parts.append(shift(block, by))
            place.append(row * along + (x - by) % along)
    return parts, jnp.stack(place)


def move_kernel(source, target, held, arrived, left):
    parts = arrived.shape[0]
    rows = held.shape[0] // parts
    spans = [pl.ds(i * rows, rows) for i in range(parts)]
    loads = start_all([(source.at[span], held.at[span]) for span in spans], arrived)
    stores = []
    for i, span in enumerate(spans):
        loads[i].wait()
        stores += start_all([(held.at[span], target.at[span])], left.at[pl.ds(i, 1)])
    for store in stores:
        store.wait()


def move(migrated):
    far = pl.BlockSpec(memory_space=pltpu.HBM)
    return pl.pallas_call(
        move_kernel,
        out_shape=jax.ShapeDtypeStruct(migrated.shape, migrated.dtype),
        in_specs=[far],
        out_specs=far,
        scratch_shapes=[
            pltpu.VMEM(migrated.shape, migrated.dtype),
            pltpu.SemaphoreType.DMA((4,)),
            pltpu.SemaphoreType.DMA((4,)),
        ],
        compiler_params=pltpu.CompilerParams(vmem_limit_bytes=60 << 20),
        cost_estimate=pl.CostEstimate(flops=0, bytes_accessed=3 << 20, transcendentals=0),
        name="move",
    )(migrated)


def send_round_ring(blocks):
    size = lax.axis_size("tp")

    def shift(block, by):
        return lax.ppermute(block, "tp", [(i, (i + by) % size) for i in range(size)])

    def total(*terms):
        return sum(term.astype(jnp.float32) for term in terms)

    half = blocks[4].shape[0] // 2
    far_up = shift(blocks[4][:half], 2)
    far_down = shift(blocks[4][half:], -2)
    up, near_up = shift(jnp.stack([blocks[3], blocks[1]]), 1)
    down, near_down = shift(jnp.stack([blocks[-3], blocks[-1]]), -1)
    above = total(blocks[2], up)
    above = jnp.concatenate([above[:half] + far_up.astype(jnp.float32), above[half:]], 0)
    below = total(blocks[-2], down)
    below = jnp.concatenate([below[:half], below[half:] + far_down.astype(jnp.float32)], 0)
    above = shift(above.astype(jnp.bfloat16), 2)
    below = shift(below.astype(jnp.bfloat16), -2)
    return blocks[0], near_up, near_down, above, below


def per_device(
    queries,
    new_token_cache,
    kv_pool,
    block_table,
    context_len,
    out_proj,
    finished_prompt_cache,
    prompt_blocks,
    prompt_tail,
    prompt_owner,
):
    receivers = lax.axis_size("grp") * lax.axis_size("seq")
    heads, packed = attend_and_pack(
        receivers,
        queries,
        new_token_cache,
        kv_pool,
        block_table,
        context_len,
        finished_prompt_cache,
        prompt_blocks,
        prompt_tail,
        prompt_owner,
    )
    parts, place = gather_heads(heads)
    migrated = lax.all_to_all(packed, ("grp", "seq"), split_axis=0, concat_axis=0, tiled=True)
    me = lax.axis_index("tp").reshape(1)
    terms = send_round_ring(dict(zip(OFFSETS, project(me, place, parts, out_proj))))
    migrated = move(migrated)
    migrated, own = lax.optimization_barrier((migrated, terms[0]))
    terms = (own,) + terms[1:]
    decoded = sum(term.astype(jnp.float32) for term in terms).astype(jnp.bfloat16)
    return (decoded, migrated)


def solution(mesh):
    placed = (
        P(None, ("grp", "seq"), "tp"),
        P(None, ("grp", "seq"), "tp"),
        P(("grp", "seq"), None, "tp"),
        P(("grp", "seq"), None),
        P(("grp", "seq"), None),
        P("tp", "seq"),
        P(("grp", "seq"), None, "tp"),
        P(("grp", "seq"), None),
        P(("grp", "seq"), None),
        P(("grp", "seq"), None),
    )
    return jax.shard_map(
        per_device,
        mesh=mesh,
        in_specs=placed,
        out_specs=(P(None, "grp", ("seq", "tp")), P(("grp", "seq"), None, "tp")),
        check_vma=False,
    )
```

```python
import jax
import jax.numpy as jnp
from jax import lax
from jax.experimental import pallas as pl
from jax.experimental.pallas import tpu as pltpu
from jax.sharding import PartitionSpec as P

HEAD_SIZE = 128
PAGE_TOKENS = 16
CAP = 3
NEGATIVE = -1e30
OFFSETS = (4, 3, -3, 2, -2, 1, -1, 0)
PROJECT_WEIGHT = 10
GROUP = 16


def start_all(copies, arrived):
    started = [
        pltpu.make_async_copy(source, target, arrived.at[i])
        for i, (source, target) in enumerate(copies)
    ]
    for copy in started:
        copy.start()
    return started


def pack_blocks(blocks, tail, owner, finished, packed):
    count = finished.shape[0]
    token = lax.broadcasted_iota(jnp.int32, finished.shape[1:], 0)
    start = jnp.int32(0)
    for j in range(blocks.shape[1]):
        held = blocks[0, j]
        for slot in range(CAP):
            valid = jnp.where(slot == held - 1, tail[0, j], PAGE_TOKENS)
            valid = jnp.where(slot < held, valid, 0)
            block = finished[jnp.minimum(start + slot, count - 1)]
            packed[owner[0, j] * CAP + slot] = jnp.where(
                token < valid, block, jnp.zeros_like(block)
            )
        start = start + held


def attend_kernel(
    blocks_hbm,
    tail_hbm,
    owner_hbm,
    finished_hbm,
    table_hbm,
    length_hbm,
    pool_hbm,
    fresh_hbm,
    queries_hbm,
    out,
    packed_hbm,
    blocks,
    tail,
    owner,
    finished,
    table,
    length,
    pool,
    fresh,
    queries,
    packed,
    key_rows,
    value_rows,
    arrived,
    left,
):
    sources = (blocks_hbm, tail_hbm, owner_hbm, finished_hbm)
    sources += (table_hbm, length_hbm, pool_hbm, fresh_hbm, queries_hbm)
    targets = (blocks, tail, owner, finished, table, length, pool, fresh, queries)
    loads = start_all(list(zip(sources, targets)), arrived)
    packed[...] = jnp.zeros_like(packed)
    steps, rows, width = queries.shape
    heads = width // HEAD_SIZE
    pages = table.shape[0]
    context = pages * PAGE_TOKENS
    cached = GROUP * context
    recent = steps * GROUP
    scale = HEAD_SIZE ** (-0.5)

    def index(columns, axis):
        return lax.broadcasted_iota(jnp.int32, (GROUP, columns), axis)

    own_cached = index(cached, 1) // context == index(cached, 0)
    cached_place = index(cached, 1) % context
    own_recent = index(recent, 1) % GROUP == index(recent, 0)
    recent_bias = [
        jnp.where(own_recent & (index(recent, 1) // GROUP <= s), 0.0, NEGATIVE)
        for s in range(steps)
    ]
    tile_row = index(cached, 0)
    for load in loads[:4]:
        load.wait()
    pack_blocks(blocks, tail, owner, finished, packed)
    (store,) = start_all([(packed, packed_hbm)], left)
    for load in loads[4:]:
        load.wait()
    groups = range(rows // GROUP)
    cached_bias = []
    for g in groups:
        first = g * GROUP
        limit = jnp.zeros((GROUP, cached), jnp.int32)
        for r in range(GROUP):
            limit = jnp.where(tile_row == r, length[0, first + r], limit)
            for j in range(pages):
                page = pool[table[j, first + r]]
                at = pl.ds(r * context + j * PAGE_TOKENS, PAGE_TOKENS)
                key_rows[g, at, :] = page[:, :HEAD_SIZE]
                value_rows[g, at, :] = page[:, HEAD_SIZE:]
        for u in range(steps):
            token = fresh[u, pl.ds(first, GROUP), :]
            at = pl.ds(cached + u * GROUP, GROUP)
            key_rows[g, at, :] = token[:, :HEAD_SIZE]
            value_rows[g, at, :] = token[:, HEAD_SIZE:]
        cached_bias.append(jnp.where(own_cached & (cached_place < limit), 0.0, NEGATIVE))
    for g in groups:
        at = pl.ds(g * GROUP, GROUP)
        scores = []
        for s in range(steps):
            query = jnp.concatenate(
                [queries[s, at, h * HEAD_SIZE : (h + 1) * HEAD_SIZE] for h in range(heads)], 0
            )
            scores.append(
                lax.dot_general(
                    query,
                    key_rows[g],
                    (((1,), (1,)), ((), ())),
                    preferred_element_type=jnp.float32,
                )
            )
        probs = []
        for s in range(steps):
            bias = jnp.concatenate([cached_bias[g], recent_bias[s]], 1)
            masked = scores[s].reshape(heads, GROUP, cached + recent) * scale + bias[None]
            raw = jnp.exp(masked - jnp.max(masked, -1, keepdims=True))
            share = raw * (1.0 / jnp.sum(raw, -1, keepdims=True))
            probs.append(share.astype(jnp.bfloat16).reshape(heads * GROUP, cached + recent))
        for s in range(steps):
            mixed = jnp.dot(probs[s], value_rows[g], preferred_element_type=jnp.float32)
            mixed = mixed.astype(jnp.bfloat16)
            for h in range(heads):
                out[s, at, h * HEAD_SIZE : (h + 1) * HEAD_SIZE] = mixed[h * GROUP : (h + 1) * GROUP]
    store.wait()


def attend_and_pack(receivers, queries, fresh, pool, table, length, finished, blocks, tail, owner):
    steps, rows, width = queries.shape
    table = table.T
    keys = GROUP * (table.shape[0] * PAGE_TOKENS + steps)
    operands = (blocks, tail, owner, finished, table, length, pool, fresh, queries)
    far = pl.BlockSpec(memory_space=pltpu.HBM)
    packed = (receivers * CAP,) + finished.shape[1:]
    return pl.pallas_call(
        attend_kernel,
        out_shape=[
            jax.ShapeDtypeStruct(queries.shape, jnp.bfloat16),
            jax.ShapeDtypeStruct(packed, finished.dtype),
        ],
        in_specs=[far] * len(operands),
        out_specs=[pl.BlockSpec(memory_space=pltpu.VMEM), far],
        scratch_shapes=[
            pltpu.SMEM(operand.shape, operand.dtype)
            if operand.dtype == jnp.int32
            else pltpu.VMEM(operand.shape, operand.dtype)
            for operand in operands
        ]
        + [
            pltpu.VMEM(packed, finished.dtype),
            pltpu.VMEM((rows // GROUP, keys, HEAD_SIZE), jnp.bfloat16),
            pltpu.VMEM((rows // GROUP, keys, HEAD_SIZE), jnp.bfloat16),
            pltpu.SemaphoreType.DMA((len(operands),)),
            pltpu.SemaphoreType.DMA((1,)),
        ],
        compiler_params=pltpu.CompilerParams(vmem_limit_bytes=60 << 20),
        cost_estimate=pl.CostEstimate(
            flops=4 * steps * rows * (width // HEAD_SIZE) * keys * HEAD_SIZE,
            bytes_accessed=5 << 20,
            transcendentals=0,
        ),
        name="attend_and_pack",
    )(*operands)


def project_kernel(me, place, *refs):
    parts = refs[: -1 - len(OFFSETS)]
    weight = refs[len(parts)]
    outs = refs[len(parts) + 1 :]
    steps, rows, width = parts[0].shape
    shares = len(OFFSETS)
    share = weight.shape[1] // shares
    lines = jnp.concatenate([part[...].reshape(steps * rows, width) for part in parts], 0)
    for at in range(0, shares, 2):
        columns = [
            weight[:, pl.ds(pl.multiple_of((me[0] + OFFSETS[at + i]) % shares * share, share), share)]
            for i in range(2)
        ]
        product = jnp.dot(
            lines, jnp.concatenate(columns, 1), preferred_element_type=jnp.float32
        ).astype(jnp.bfloat16)
        product = product.reshape(len(parts), steps, rows, 2 * share)
        for q in range(len(parts)):
            to = pl.ds(pl.multiple_of(place[q] * rows, rows), rows)
            for i in range(2):
                outs[at + i][:, to, :] = product[q, :, :, i * share : (i + 1) * share]


def project(me, place, parts, weight):
    steps, rows, width = parts[0].shape
    columns = weight.shape[1]
    share = columns // len(OFFSETS)
    smem = pl.BlockSpec(memory_space=pltpu.SMEM)
    vmem = pl.BlockSpec(memory_space=pltpu.VMEM)
    block = jax.ShapeDtypeStruct((steps, len(parts) * rows, share), jnp.bfloat16)
    return pl.pallas_call(
        project_kernel,
        out_shape=[block] * len(OFFSETS),
        in_specs=[smem, smem] + [vmem] * (len(parts) + 1),
        out_specs=[vmem] * len(OFFSETS),
        compiler_params=pltpu.CompilerParams(vmem_limit_bytes=32 << 20),
        cost_estimate=pl.CostEstimate(
            flops=PROJECT_WEIGHT * 2 * len(parts) * steps * rows * width * columns,
            bytes_accessed=6 << 20,
            transcendentals=0,
        ),
        name="project",
    )(me, place, *parts, weight)


def gather_heads(heads):
    across, along = 2, lax.axis_size("seq") // 2

    def shift(block, by):
        pairs = [(z * along + x, z * along + (x + by) % along) for z in range(across) for x in range(along)]
        return lax.ppermute(block, "seq", pairs)

    me = lax.axis_index("seq")
    z, x = me // along, me % along
    other = lax.ppermute(heads, "seq", [(i, (i + along) % (2 * along)) for i in range(2 * along)])
    parts, place = [heads, other], [me, (1 - z) * along + x]
    for row, block in ((z, heads), (1 - z, other)):
        for by in ((2, -1, 1) if block is heads else (1, -1, 2)):
            parts.append(shift(block, by))
            place.append(row * along + (x - by) % along)
    return parts, jnp.stack(place)


def move_kernel(source, target, held, arrived, left):
    parts = arrived.shape[0]
    rows = held.shape[0] // parts
    spans = [pl.ds(i * rows, rows) for i in range(parts)]
    loads = start_all([(source.at[span], held.at[span]) for span in spans], arrived)
    stores = []
    for i, span in enumerate(spans):
        loads[i].wait()
        stores += start_all([(held.at[span], target.at[span])], left.at[pl.ds(i, 1)])
    for store in stores:
        store.wait()


def move(migrated):
    far = pl.BlockSpec(memory_space=pltpu.HBM)
    return pl.pallas_call(
        move_kernel,
        out_shape=jax.ShapeDtypeStruct(migrated.shape, migrated.dtype),
        in_specs=[far],
        out_specs=far,
        scratch_shapes=[
            pltpu.VMEM(migrated.shape, migrated.dtype),
            pltpu.SemaphoreType.DMA((4,)),
            pltpu.SemaphoreType.DMA((4,)),
        ],
        compiler_params=pltpu.CompilerParams(vmem_limit_bytes=60 << 20),
        cost_estimate=pl.CostEstimate(flops=0, bytes_accessed=3 << 20, transcendentals=0),
        name="move",
    )(migrated)


def send_round_ring(blocks):
    size = lax.axis_size("tp")

    def shift(block, by):
        return lax.ppermute(block, "tp", [(i, (i + by) % size) for i in range(size)])

    def total(*terms):
        return sum(term.astype(jnp.float32) for term in terms)

    half = blocks[4].shape[0] // 2
    far_up = shift(blocks[4][:half], 2)
    far_down = shift(blocks[4][half:], -2)
    up, near_up = shift(jnp.stack([blocks[3], blocks[1]]), 1)
    down, near_down = shift(jnp.stack([blocks[-3], blocks[-1]]), -1)
    above = total(blocks[2], up)
    above = jnp.concatenate([above[:half] + far_up.astype(jnp.float32), above[half:]], 0)
    below = total(blocks[-2], down)
    below = jnp.concatenate([below[:half], below[half:] + far_down.astype(jnp.float32)], 0)
    above = shift(above.astype(jnp.bfloat16), 2)
    below = shift(below.astype(jnp.bfloat16), -2)
    return blocks[0], near_up, near_down, above, below


def per_device(
    queries,
    new_token_cache,
    kv_pool,
    block_table,
    context_len,
    out_proj,
    finished_prompt_cache,
    prompt_blocks,
    prompt_tail,
    prompt_owner,
):
    receivers = lax.axis_size("grp") * lax.axis_size("seq")
    heads, packed = attend_and_pack(
        receivers,
        queries,
        new_token_cache,
        kv_pool,
        block_table,
        context_len,
        finished_prompt_cache,
        prompt_blocks,
        prompt_tail,
        prompt_owner,
    )
    parts, place = gather_heads(heads)
    migrated = lax.all_to_all(packed, ("grp", "seq"), split_axis=0, concat_axis=0, tiled=True)
    me = lax.axis_index("tp").reshape(1)
    terms = send_round_ring(dict(zip(OFFSETS, project(me, place, parts, out_proj))))
    migrated = move(migrated)
    migrated, own = lax.optimization_barrier((migrated, terms[0]))
    terms = (own,) + terms[1:]
    decoded = sum(term.astype(jnp.float32) for term in terms).astype(jnp.bfloat16)
    return (decoded, migrated)


def solution(mesh):
    placed = (
        P(None, ("grp", "seq"), "tp"),
        P(None, ("grp", "seq"), "tp"),
        P(("grp", "seq"), None, "tp"),
        P(("grp", "seq"), None),
        P(("grp", "seq"), None),
        P("tp", "seq"),
        P(("grp", "seq"), None, "tp"),
        P(("grp", "seq"), None),
        P(("grp", "seq"), None),
        P(("grp", "seq"), None),
    )
    return jax.shard_map(
        per_device,
        mesh=mesh,
        in_specs=placed,
        out_specs=(P(None, "grp", ("seq", "tp")), P(("grp", "seq"), None, "tp")),
        check_vma=False,
    )
```
